32 devices in a mesh: line: 8 (over y, x, core), seg: 4 (over z).
Axes of the slice: x: 2, y: 2, z: 4, core: 2. Of those that a mesh axis runs over, the one named last changes fastest.
Arguments:
- right_side: float32 [8, 32, 96, 128], P('line', 'seg'), may hold values from -24 to 24
- band_blocks: bfloat16 [8, 32, 4, 96, 96], P('line', 'seg')
- knot_pairs: int32 [8, 4, 6, 2, 2], P('line', 'seg'), may hold values from 0 to 7
- pair_counts: int32 [8, 4, 6], P('line', 'seg'), may hold values from 1 to 2, as said below
- cross_blocks: bfloat16 [8, 4, 6, 2, 96, 96], P('line', 'seg'), may hold values from -0.359375 to 0.359375
Outputs:
- solution: float32 [8, 32, 96, 128], P('line', 'seg')
The draws below stay inside these ranges and needn't reach their ends.
Inputs may be any that keep to these rules, and one draw needn't show every extreme that they name: `knot_pairs`: entry s of bucket b counts only if s < pair_counts of that bucket; other entries are unused. `pair_counts`: every bucket holds at least one pair, and in every draw some line and segment has all buckets full.
All inputs are finite; a program needn't handle non-finite values.
Results may differ from the reference program's by a relative error of at most 0.0028.
Values may be sent and summed in bfloat16 or wider, within the bound.
A program may use at most 64 MiB of HBM per device.

```python
import math
import jax
import jax.numpy as jnp
from jax import lax

PARAMS = 96
PROBES = 128
KNOT_DEV = 8
GROUP = 4
CAP = 2
ITERS = 3
LINES = 8
SEGS = 4
KNOTS = 32
BUCKETS = 6


def band_sample(line_key):
    shape = (KNOTS, 4, PARAMS, PARAMS)
    sigma = 0.4 / math.sqrt(PARAMS)
    base = jax.random.normal(line_key, shape, jnp.float32) * sigma
    levels = jnp.exp(jax.random.uniform(jax.random.fold_in(line_key, 7), (KNOTS, PARAMS), jnp.float32, math.log(4.0), math.log(8.0)))
    first = base[:, 0]
    symmetric = (first + jnp.swapaxes(first, -1, -2)) * 0.70710678
    eye_block = jnp.eye(PARAMS, dtype=jnp.float32)
    diag_block = symmetric + levels[:, :, None] * eye_block
    return base.at[:, 0].set(diag_block)


def draw_band_blocks(key, part):
    line_keys = jax.vmap(lambda index: jax.random.fold_in(key, index))(jnp.arange(LINES))
    whole = lax.map(band_sample, line_keys)
    return whole.astype(jnp.bfloat16)


def draw_pair_counts(key, part):
    base = jax.random.randint(key, (LINES, SEGS, BUCKETS), 1, CAP + 1, jnp.int32)
    pick_line = jax.random.randint(jax.random.fold_in(key, 1), (), 0, LINES, jnp.int32)
    pick_seg = jax.random.randint(jax.random.fold_in(key, 2), (), 0, SEGS, jnp.int32)
    chosen = (jnp.arange(LINES, dtype=jnp.int32)[:, None] == pick_line) & (jnp.arange(SEGS, dtype=jnp.int32)[None, :] == pick_seg)
    base = jnp.where(chosen[:, :, None], CAP, base)
    return base.astype(jnp.int32)


def set_ends(entries, own_key, low, high):
    spot = [jax.random.randint(jax.random.fold_in(own_key, axis), (), 0, length) for axis, length in enumerate(entries.shape)]
    widest = entries.shape.index(max(entries.shape))
    neighbour = spot[:widest] + [(spot[widest] + 1) % entries.shape[widest]] + spot[widest + 1:]
    return entries.at[tuple(spot)].set(low).at[tuple(neighbour)].set(high)


def block_scale(stream_key, extent, pieces, least, top_value):
    def one(position, parts):
        draws = jax.random.uniform(jax.random.fold_in(jax.random.fold_in(stream_key, 6), position), (parts,), jnp.float32, least / len(pieces), top_value / len(pieces))
        return jnp.repeat(jnp.exp(draws), extent[position] // parts).reshape((-1,) + (1,) * (len(extent) - position - 1))

    gain = one(*pieces[0])
    for cut in pieces[1:]:
        gain = gain * one(*cut)
    return gain


def gaussian(own_key, shape, spread, bound, cuts=(), held_as=jnp.bfloat16):
    loudness = block_scale(own_key, shape, cuts, -0.22, 0.18) if cuts else 1.0
    entries = jax.random.normal(own_key, shape, jnp.float32) * spread * loudness
    return jnp.minimum(jnp.maximum(entries, -bound), bound).astype(held_as)


def setup_inputs(seed: int = 0) -> dict:
    splits = jax.random.split(jax.random.key(seed), 6)
    right_side = gaussian(splits[0], (LINES, KNOTS, PARAMS, PROBES), 4.0, 24.0, ((0, 8), (1, 4)), jnp.float32)
    band_blocks = draw_band_blocks(jax.random.fold_in(splits[5], 71), 0)
    knot_pairs = set_ends(jax.random.randint(splits[2], (LINES, SEGS, BUCKETS, CAP, 2), 0, KNOT_DEV), jax.random.fold_in(splits[2], 1), 0, KNOT_DEV - 1).astype(jnp.int32)
    pair_counts = draw_pair_counts(jax.random.fold_in(splits[5], 71), 0)
    cross_blocks = gaussian(splits[4], (LINES, SEGS, BUCKETS, CAP, PARAMS, PARAMS), 0.06, 0.359375, ((0, 8), (1, 4)))
    return dict(right_side=right_side, band_blocks=band_blocks, knot_pairs=knot_pairs, pair_counts=pair_counts, cross_blocks=cross_blocks)


LO_BOUND = 1.5
HI_BOUND = 12.0


def bucket_offsets():
    return [b - (GROUP - 1) if b < GROUP - 1 else b - GROUP + 2 for b in range(BUCKETS)]


def band_apply(line_blocks, search_vector):
    blocks = line_blocks.astype(jnp.float32)
    padded = jnp.pad(search_vector, ((3, 3), (0, 0), (0, 0)))
    summed = jnp.zeros(search_vector.shape, jnp.float32)
    for step in range(4):
        summed = summed + jnp.einsum('kab,kbr->kar', blocks[:, step], padded[3 + step:3 + step + KNOTS], precision=lax.Precision.HIGHEST)
    for step in range(1, 4):
        lower_term = jnp.einsum('kba,kbr->kar', blocks[:KNOTS - step, step], search_vector[:KNOTS - step], precision=lax.Precision.HIGHEST)
        summed = summed + jnp.pad(lower_term, ((step, 0), (0, 0), (0, 0)))
    return summed


def operator(probe_bf, band_blocks, knot_pairs, pair_counts, cross_blocks):
    search_vector = probe_bf.astype(jnp.float32)
    iterate_output = lax.map(lambda pair: band_apply(pair[0], pair[1]), (band_blocks, search_vector))
    offsets = bucket_offsets()
    line_ids = jnp.arange(LINES).astype(jnp.int32)[:, None, None]
    seg_ids = jnp.arange(SEGS).astype(jnp.int32)[None, :, None]
    slot_ids = jnp.arange(CAP).astype(jnp.int32)[None, None, :]
    zeros_idx = jnp.zeros((LINES, SEGS, CAP), jnp.int32)
    for bucket in range(BUCKETS):
        occupied_mask = slot_ids < pair_counts[:, :, bucket][..., None]
        home_knot = (seg_ids * KNOT_DEV + knot_pairs[:, :, bucket, :, 0]).astype(jnp.int32)
        far_knot = (seg_ids * KNOT_DEV + knot_pairs[:, :, bucket, :, 1]).astype(jnp.int32)
        home_line = (line_ids + zeros_idx).astype(jnp.int32)
        far_line = ((line_ids + offsets[bucket] + LINES) % LINES).astype(jnp.int32) + zeros_idx
        weight = occupied_mask.astype(jnp.float32)[..., None, None]
        blocks = cross_blocks[:, :, bucket].astype(jnp.float32)
        far_vec = search_vector[far_line, far_knot]
        home_vec = search_vector[home_line, home_knot]
        forward = jnp.einsum('lscab,lscbr->lscar', blocks, far_vec, precision=lax.Precision.HIGHEST) * weight
        backward = jnp.einsum('lscba,lscbr->lscar', blocks, home_vec, precision=lax.Precision.HIGHEST) * weight
        iterate_output = iterate_output.at[home_line, home_knot].add(forward)
        iterate_output = iterate_output.at[far_line, far_knot].add(backward)
    return iterate_output


def reference(right_side, band_blocks, knot_pairs, pair_counts, cross_blocks):
    center = (HI_BOUND + LO_BOUND) / 2.0
    radius = (HI_BOUND - LO_BOUND) / 2.0
    coeff = radius / center
    solution = jnp.zeros(right_side.shape, jnp.float32)
    residual = right_side
    direction = right_side / center
    for turn in range(ITERS):
        probe_bf = direction.astype(jnp.bfloat16)
        solution = solution + direction
        residual = residual - operator(probe_bf, band_blocks, knot_pairs, pair_counts, cross_blocks)
        coeff_next = 1.0 / (2.0 * center / radius - coeff)
        direction = (coeff_next * coeff) * direction + (2.0 * coeff_next / radius) * residual
        coeff = coeff_next
    return solution + direction
```

```python
import functools

import jax
import jax.numpy as jnp
from jax import lax
from jax.experimental import pallas as pl
from jax.experimental.pallas import tpu as pltpu
from jax.sharding import PartitionSpec as P

ITERS = 3
HALO = 3
LO_BOUND = 1.5
HI_BOUND = 12.0
MESH = pl.DeviceIdType.MESH


def kernel(lines, segs, offsets, slots, *refs):
    (meta_ref, meta_vec, rhs, band, cross, out) = refs[:6]
    (wide, cmask, ctrans, lower, meta_in, meta_far, resid, direc) = refs[6:14]
    per = [refs[14 + 6 * t : 20 + 6 * t] for t in range(ITERS)]
    send_sem, recv_sem, local_sem = refs[14 + 6 * ITERS :]
    knots, params, probes = rhs.shape
    buckets = len(offsets)
    line = lax.axis_index("line")
    seg = lax.axis_index("seg")
    has_prev = seg > 0
    has_next = seg < segs - 1

    def line_at(shift):
        return (lax.rem(line + (shift + lines), lines), seg)

    prev_dev = (line, jnp.maximum(seg - 1, 0))
    next_dev = (line, jnp.minimum(seg + 1, segs - 1))

    barrier = pltpu.get_barrier_semaphore()
    for off in offsets:
        pl.semaphore_signal(barrier, inc=1, device_id=line_at(off), device_id_type=MESH)

    @pl.when(has_prev)
    def _():
        pl.semaphore_signal(barrier, inc=1, device_id=prev_dev, device_id_type=MESH)

    @pl.when(has_next)
    def _():
        pl.semaphore_signal(barrier, inc=1, device_id=next_dev, device_id_type=MESH)

    center = (HI_BOUND + LO_BOUND) / 2.0
    radius = (HI_BOUND - LO_BOUND) / 2.0
    coeff = radius / center

    for k in range(knots):
        first = rhs[k] / center
        direc[k] = first
        resid[k] = rhs[k]
        out[k] = first
        per[0][0][k] = first.astype(jnp.bfloat16)

    pl.semaphore_wait(
        barrier, buckets + has_prev.astype(jnp.int32) + has_next.astype(jnp.int32)
    )

    def remote(src, dst, sem, device):
        return pltpu.make_async_remote_copy(
            src_ref=src,
            dst_ref=dst,
            send_sem=send_sem.at[sem],
            recv_sem=recv_sem.at[sem],
            device_id=device,
            device_id_type=MESH,
        )

    meta_copies = [
        remote(meta_vec, meta_in.at[b], b, line_at(off)) for b, off in enumerate(offsets)
    ]
    for copy in meta_copies:
        copy.start()
    lower_copy = remote(band.at[pl.ds(knots - HALO, HALO)], lower, buckets, next_dev)
    base = buckets + 1
    stride = 2 * buckets + 2

    def halo_copies(t):
        own, ext = per[t][0], per[t][1]
        at = base + t * stride
        up = remote(own.at[pl.ds(knots - HALO, HALO)], ext.at[pl.ds(0, HALO)], at, next_dev)
        down = remote(own.at[pl.ds(0, HALO)], ext.at[pl.ds(HALO + knots, HALO)], at + 1, prev_dev)
        return up, down

    def start_halos(t):
        up, down = halo_copies(t)

        @pl.when(has_next)
        def _():
            up.start()

        @pl.when(has_prev)
        def _():
            down.start()

    start_halos(0)

    @pl.when(has_next)
    def _():
        lower_copy.start()

    def own_index(b, s, which):
        return meta_ref[0, (b * slots + s) * 2 + which]

    def far_index(b, s):
        return meta_far[b, 0, (b * slots + s) * 2 + 1]

    for b in range(buckets):
        for s in range(slots):
            keep = (s < meta_ref[0, buckets * slots * 2 + b]).astype(jnp.float32)
            block = cross[b * slots + s].astype(jnp.float32) * keep
            cmask[b * slots + s] = block.astype(jnp.bfloat16)
            ctrans[b * slots + s] = block.T.astype(jnp.bfloat16)

    for copy in meta_copies:
        copy.wait_recv()
    to_scalar = pltpu.make_async_copy(meta_in, meta_far, local_sem)
    to_scalar.start()
    to_scalar.wait()

    def start_partners(t):
        own, _, sent_v, sent_p, got_v, got_p = per[t]
        at = base + t * stride + 2
        copies_v, copies_p = [], []
        for b, off in enumerate(offsets):
            for s in range(slots):
                sent_v[b, s] = own[far_index(b, s)]
            copy = remote(sent_v.at[b], got_v.at[b], at + b, line_at(-off))
            copy.start()
            copies_v.append(copy)
        for b, off in enumerate(offsets):
            for s in range(slots):
                sent_p[b, s] = jnp.dot(
                    ctrans[b * slots + s],
                    own[own_index(b, s, 0)],
                    preferred_element_type=jnp.float32,
                ).astype(jnp.bfloat16)
            copy = remote(sent_p.at[b], got_p.at[b], at + buckets + b, line_at(off))
            copy.start()
            copies_p.append(copy)
        return copies_v, copies_p

    partner_copies = start_partners(0)

    @pl.when(has_prev)
    def _():
        lower_copy.wait_recv()

    @pl.when(jnp.logical_not(has_prev))
    def _():
        lower[...] = jnp.zeros_like(lower)

    for k in range(knots):
        for step in range(HALO + 1):
            at = (HALO + step) * params
            wide[k, :, at : at + params] = band[k, step]
        for step in range(1, HALO + 1):
            at = (HALO - step) * params
            source = band[k - step, step] if k >= step else lower[HALO + k - step, step]
            wide[k, :, at : at + params] = source.astype(jnp.float32).T.astype(jnp.bfloat16)

    all_partner = []
    for t in range(ITERS):
        own, ext, sent_v, sent_p, got_v, got_p = per[t]
        copies_v, copies_p = partner_copies
        all_partner += copies_v + copies_p
        up, down = halo_copies(t)
        ext[pl.ds(HALO, knots)] = own[...]

        @pl.when(has_prev)
        def _():
            up.wait_recv()

        @pl.when(jnp.logical_not(has_prev))
        def _():
            ext[pl.ds(0, HALO)] = jnp.zeros((HALO, params, probes), jnp.bfloat16)

        @pl.when(has_next)
        def _():
            down.wait_recv()

        @pl.when(jnp.logical_not(has_next))
        def _():
            ext[pl.ds(HALO + knots, HALO)] = jnp.zeros((HALO, params, probes), jnp.bfloat16)

        for k in range(knots):
            near = ext[pl.ds(k, 2 * HALO + 1)].reshape((2 * HALO + 1) * params, probes)
            resid[k] = resid[k] - jnp.dot(wide[k], near, preferred_element_type=jnp.float32)

        def scatter(entries, targets):
            for k in range(knots):
                total = resid[k]
                for entry, target in zip(entries, targets):
                    total = total - jnp.where(target == k, entry, 0.0)
                resid[k] = total

        for b in range(buckets):
            copies_v[b].wait_recv()
            entries = [
                jnp.dot(
                    cmask[b * slots + s], got_v[b, s], preferred_element_type=jnp.float32
                )
                for s in range(slots)
            ]
            scatter(entries, [own_index(b, s, 0) for s in range(slots)])
        for b in range(buckets):
            copies_p[b].wait_recv()
            scatter(
                [got_p[b, s].astype(jnp.float32) for s in range(slots)],
                [far_index(b, s) for s in range(slots)],
            )
        coeff_next = 1.0 / (2.0 * center / radius - coeff)
        for k in range(knots):
            fresh = (coeff_next * coeff) * direc[k] + (2.0 * coeff_next / radius) * resid[k]
            direc[k] = fresh
            out[k] = out[k] + fresh
            if t + 1 < ITERS:
                per[t + 1][0][k] = fresh.astype(jnp.bfloat16)
        coeff = coeff_next
        if t + 1 < ITERS:
            start_halos(t + 1)
            partner_copies = start_partners(t + 1)

    for copy in meta_copies + all_partner:
        copy.wait_send()

    @pl.when(has_next)
    def _():
        lower_copy.wait_send()
        for t in range(ITERS):
            halo_copies(t)[0].wait_send()

    @pl.when(has_prev)
    def _():
        for t in range(ITERS):
            halo_copies(t)[1].wait_send()


def body(lines, segs, right_side, band_blocks, knot_pairs, pair_counts, cross_blocks):
    rhs = right_side[0]
    band = band_blocks[0]
    pairs = knot_pairs[0, 0]
    buckets, slots = pairs.shape[:2]
    knots, params, probes = rhs.shape
    cross = cross_blocks.reshape(buckets * slots, params, params)
    group = buckets // 2 + 1
    offsets = [b - (group - 1) if b < group - 1 else b - group + 2 for b in range(buckets)]
    words = jnp.concatenate(
        [jnp.clip(pairs, 0, knots - 1).reshape(-1), pair_counts.reshape(-1)]
    )
    meta = jnp.pad(words, (0, 128 - words.shape[0]))[None]
    meta_vec = jnp.broadcast_to(meta, (8, 128))
    half = jnp.bfloat16
    per = [
        pltpu.VMEM((knots, params, probes), half),
        pltpu.VMEM((knots + 2 * HALO, params, probes), half),
        pltpu.VMEM((buckets, slots, params, probes), half),
        pltpu.VMEM((buckets, slots, params, probes), half),
        pltpu.VMEM((buckets, slots, params, probes), half),
        pltpu.VMEM((buckets, slots, params, probes), half),
    ]
    sems = buckets + 1 + ITERS * (2 * buckets + 2)
    vmem = pl.BlockSpec(memory_space=pltpu.VMEM)
    smem = pl.BlockSpec(memory_space=pltpu.SMEM)
    done = pl.pallas_call(
        functools.partial(kernel, lines, segs, offsets, slots),
        out_shape=jax.ShapeDtypeStruct(rhs.shape, jnp.float32),
        in_specs=[smem, vmem, vmem, vmem, vmem],
        out_specs=vmem,
        scratch_shapes=[
            pltpu.VMEM((knots, params, (2 * HALO + 1) * params), half),
            pltpu.VMEM((buckets * slots, params, params), half),
            pltpu.VMEM((buckets * slots, params, params), half),
            pltpu.VMEM((HALO, HALO + 1, params, params), half),
            pltpu.VMEM((buckets, 8, 128), jnp.int32),
            pltpu.SMEM((buckets, 8, 128), jnp.int32),
            pltpu.VMEM(rhs.shape, jnp.float32),
            pltpu.VMEM(rhs.shape, jnp.float32),
            *(per * ITERS),
            pltpu.SemaphoreType.DMA((sems,)),
            pltpu.SemaphoreType.DMA((sems,)),
            pltpu.SemaphoreType.DMA,
        ],
        compiler_params=pltpu.CompilerParams(
            collective_id=0, has_side_effects=True, vmem_limit_bytes=32 * 2**20
        ),
        name="chebyshev",
    )(meta, meta_vec, rhs, band, cross)
    return done[None]


def solution(mesh):
    return jax.shard_map(
        functools.partial(body, mesh.shape["line"], mesh.shape["seg"]),
        mesh=mesh,
        in_specs=(
            P("line", "seg", None, None),
            P("line", "seg", None, None, None),
            P("line", "seg", None, None, None),
            P("line", "seg", None),
            P("line", "seg", None, None, None, None),
        ),
        out_specs=P("line", "seg", None, None),
        check_vma=False,
    )
```

```python
import functools

import jax
import jax.numpy as jnp
from jax import lax
from jax.experimental import pallas as pl
from jax.experimental.pallas import tpu as pltpu
from jax.sharding import PartitionSpec as P

ITERS = 3
HALO = 3
LO_BOUND = 1.5
HI_BOUND = 12.0
MESH = pl.DeviceIdType.MESH


def kernel(lines, segs, offsets, slots, *refs):
    (count_ref, meta_vec, rhs, band_in, cross_in, out) = refs[:6]
    (wide, band, cross, ctrans, lower, meta_in, meta_far, meta_own, resid, direc) = refs[6:16]
    per = [refs[16 + 6 * t : 22 + 6 * t] for t in range(ITERS)]
    send_sem, recv_sem, local_sem = refs[16 + 6 * ITERS :]
    knots, params, probes = resid.shape
    buckets = len(offsets)
    line = lax.axis_index("line")
    seg = lax.axis_index("seg")
    has_prev = seg > 0
    has_next = seg < segs - 1

    def line_at(shift):
        return (lax.rem(line + (shift + lines), lines), seg)

    prev_dev = (line, jnp.maximum(seg - 1, 0))
    next_dev = (line, jnp.minimum(seg + 1, segs - 1))

    barrier = pltpu.get_barrier_semaphore()
    for off in offsets:
        pl.semaphore_signal(barrier, inc=1, device_id=line_at(off), device_id_type=MESH)

    @pl.when(has_prev)
    def _():
        pl.semaphore_signal(barrier, inc=1, device_id=prev_dev, device_id_type=MESH)

    @pl.when(has_next)
    def _():
        pl.semaphore_signal(barrier, inc=1, device_id=next_dev, device_id_type=MESH)

    load_rhs = pltpu.make_async_copy(rhs, resid, local_sem.at[0])
    load_cross = pltpu.make_async_copy(cross_in, cross, local_sem.at[1])
    load_band = pltpu.make_async_copy(band_in, band, local_sem.at[2])
    load_own = pltpu.make_async_copy(meta_vec, meta_own, local_sem.at[3])
    load_rhs.start()
    load_own.start()
    load_cross.start()
    load_band.start()

    center = (HI_BOUND + LO_BOUND) / 2.0
    radius = (HI_BOUND - LO_BOUND) / 2.0
    coeff = radius / center

    load_rhs.wait()
    for k in range(knots):
        first = resid[k] / center
        direc[k] = first
        out[k] = first
        per[0][0][k] = first.astype(jnp.bfloat16)

    pl.semaphore_wait(
        barrier, buckets + has_prev.astype(jnp.int32) + has_next.astype(jnp.int32)
    )

    def remote(src, dst, sem, device):
        return pltpu.make_async_remote_copy(
            src_ref=src,
            dst_ref=dst,
            send_sem=send_sem.at[sem],
            recv_sem=recv_sem.at[sem],
            device_id=device,
            device_id_type=MESH,
        )

    meta_copies = [
        remote(meta_vec, meta_in.at[b], b, line_at(off)) for b, off in enumerate(offsets)
    ]
    for copy in meta_copies:
        copy.start()
    lower_copy = remote(band_in.at[pl.ds(knots - HALO, HALO)], lower, buckets, next_dev)
    base = buckets + 1
    stride = 2 * buckets + 2

    def halo_copies(t):
        own, ext = per[t][0], per[t][1]
        at = base + t * stride
        up = remote(own.at[pl.ds(knots - HALO, HALO)], ext.at[pl.ds(0, HALO)], at, next_dev)
        down = remote(own.at[pl.ds(0, HALO)], ext.at[pl.ds(HALO + knots, HALO)], at + 1, prev_dev)
        return up, down

    def start_halos(t):
        up, down = halo_copies(t)

        @pl.when(has_next)
        def _():
            up.start()

        @pl.when(has_prev)
        def _():
            down.start()

    def own_index(b, s, which):
        return jnp.clip(meta_own[0, (b * slots + s) * 2 + which], 0, knots - 1)

    def far_index(b, s):
        return jnp.clip(meta_far[b, 0, (b * slots + s) * 2 + 1], 0, knots - 1)

    def asked_copies(t):
        at = base + t * stride + 2
        return [
            remote(per[t][2].at[b], per[t][4].at[b], at + b, line_at(-off))
            for b, off in enumerate(offsets)
        ]

    def product_copies(t):
        at = base + t * stride + 2 + buckets
        return [
            remote(per[t][3].at[b], per[t][5].at[b], at + b, line_at(off))
            for b, off in enumerate(offsets)
        ]

    def start_asked(t):
        for b, copy in enumerate(asked_copies(t)):
            for s in range(slots):
                per[t][2][b, s] = per[t][0][far_index(b, s)]
            copy.start()

    def start_products(t):
        for b, copy in enumerate(product_copies(t)):
            for s in range(slots):
                if t == 0:
                    keep = s < count_ref[b]
                    block = cross[b * slots + s]
                    block = jnp.where(keep, block, jnp.zeros_like(block))
                    cross[b * slots + s] = block
                    ctrans[b * slots + s] = block.T
                per[t][3][b, s] = jnp.dot(
                    ctrans[b * slots + s],
                    per[t][0][own_index(b, s, 0)],
                    preferred_element_type=jnp.float32,
                ).astype(jnp.bfloat16)
            copy.start()

    start_halos(0)

    @pl.when(has_next)
    def _():
        lower_copy.start()

    load_own.wait()
    load_cross.wait()
    start_products(0)
    for copy in meta_copies:
        copy.wait_recv()
    to_scalar = pltpu.make_async_copy(meta_in, meta_far, local_sem.at[4])
    to_scalar.start()
    to_scalar.wait()
    start_asked(0)

    load_band.wait()
    for k in range(knots):
        for step in range(HALO + 1):
            at = (HALO + step) * params
            wide[k, :, at : at + params] = band[k, step]
        for step in range(1, min(k, HALO) + 1):
            at = (HALO - step) * params
            wide[k, :, at : at + params] = band[k - step, step].T

    @pl.when(has_prev)
    def _():
        lower_copy.wait_recv()

    @pl.when(jnp.logical_not(has_prev))
    def _():
        lower[...] = jnp.zeros_like(lower)

    for k in range(HALO):
        for step in range(k + 1, HALO + 1):
            at = (HALO - step) * params
            wide[k, :, at : at + params] = lower[HALO + k - step, step].T

    for t in range(ITERS):
        own, ext, sent_v, sent_p, got_v, got_p = per[t]
        up, down = halo_copies(t)
        ext[pl.ds(HALO, knots)] = own[...]

        @pl.when(has_prev)
        def _():
            up.wait_recv()

        @pl.when(jnp.logical_not(has_prev))
        def _():
            ext[pl.ds(0, HALO)] = jnp.zeros((HALO, params, probes), jnp.bfloat16)

        @pl.when(has_next)
        def _():
            down.wait_recv()

        @pl.when(jnp.logical_not(has_next))
        def _():
            ext[pl.ds(HALO + knots, HALO)] = jnp.zeros((HALO, params, probes), jnp.bfloat16)

        for k in range(knots):
            near = ext[pl.ds(k, 2 * HALO + 1)].reshape((2 * HALO + 1) * params, probes)
            resid[k] = resid[k] - jnp.dot(wide[k], near, preferred_element_type=jnp.float32)

        def scatter(entries, targets):
            for k in range(knots):
                total = resid[k]
                for entry, target in zip(entries, targets):
                    total = total - jnp.where(target == k, entry, 0.0)
                resid[k] = total

        def add_asked():
            for b, copy in enumerate(asked_copies(t)):
                copy.wait_recv()
                entries = [
                    jnp.dot(
                        cross[b * slots + s], got_v[b, s], preferred_element_type=jnp.float32
                    )
                    for s in range(slots)
                ]
                scatter(entries, [own_index(b, s, 0) for s in range(slots)])

        def add_products():
            for b, copy in enumerate(product_copies(t)):
                copy.wait_recv()
                scatter(
                    [got_p[b, s].astype(jnp.float32) for s in range(slots)],
                    [far_index(b, s) for s in range(slots)],
                )

        if t == 0:
            add_products()
            add_asked()
        else:
            add_asked()
            add_products()
        coeff_next = 1.0 / (2.0 * center / radius - coeff)
        for k in range(knots):
            fresh = (coeff_next * coeff) * direc[k] + (2.0 * coeff_next / radius) * resid[k]
            out[k] = out[k] + fresh
            if t + 1 < ITERS:
                direc[k] = fresh
                per[t + 1][0][k] = fresh.astype(jnp.bfloat16)
        coeff = coeff_next
        if t + 1 < ITERS:
            start_halos(t + 1)
            start_asked(t + 1)
            start_products(t + 1)

    for copy in meta_copies:
        copy.wait_send()
    for t in range(ITERS):
        for copy in asked_copies(t) + product_copies(t):
            copy.wait_send()

    @pl.when(has_next)
    def _():
        lower_copy.wait_send()
        for t in range(ITERS):
            halo_copies(t)[0].wait_send()

    @pl.when(has_prev)
    def _():
        for t in range(ITERS):
            halo_copies(t)[1].wait_send()


def body(lines, segs, right_side, band_blocks, knot_pairs, pair_counts, cross_blocks):
    rhs = right_side[0]
    band = band_blocks[0]
    pairs = knot_pairs[0, 0]
    buckets, slots = pairs.shape[:2]
    knots, params, probes = rhs.shape
    cross = cross_blocks.reshape(buckets * slots, params, params)
    group = buckets // 2 + 1
    offsets = [b - (group - 1) if b < group - 1 else b - group + 2 for b in range(buckets)]
    words = pairs.reshape(-1)
    meta = jnp.pad(words, (0, 128 - words.shape[0]))[None]
    half = jnp.bfloat16
    per = [
        pltpu.VMEM((knots, params, probes), half),
        pltpu.VMEM((knots + 2 * HALO, params, probes), half),
        pltpu.VMEM((buckets, slots, params, probes), half),
        pltpu.VMEM((buckets, slots, params, probes), half),
        pltpu.VMEM((buckets, slots, params, probes), half),
        pltpu.VMEM((buckets, slots, params, probes), half),
    ]
    sems = buckets + 1 + ITERS * (2 * buckets + 2)
    vmem = pl.BlockSpec(memory_space=pltpu.VMEM)
    hbm = pl.BlockSpec(memory_space=pltpu.HBM)
    smem = pl.BlockSpec(memory_space=pltpu.SMEM)
    done = pl.pallas_call(
        functools.partial(kernel, lines, segs, offsets, slots),
        out_shape=jax.ShapeDtypeStruct(rhs.shape, jnp.float32),
        in_specs=[smem, vmem, hbm, hbm, hbm],
        out_specs=vmem,
        scratch_shapes=[
            pltpu.VMEM((knots, params, (2 * HALO + 1) * params), half),
            pltpu.VMEM(band.shape, half),
            pltpu.VMEM(cross.shape, half),
            pltpu.VMEM(cross.shape, half),
            pltpu.VMEM((HALO, HALO + 1, params, params), half),
            pltpu.VMEM((buckets, 1, 128), jnp.int32),
            pltpu.SMEM((buckets, 1, 128), jnp.int32),
            pltpu.SMEM((1, 128), jnp.int32),
            pltpu.VMEM(rhs.shape, jnp.float32),
            pltpu.VMEM(rhs.shape, jnp.float32),
            *(per * ITERS),
            pltpu.SemaphoreType.DMA((sems,)),
            pltpu.SemaphoreType.DMA((sems,)),
            pltpu.SemaphoreType.DMA((5,)),
        ],
        compiler_params=pltpu.CompilerParams(
            collective_id=0, has_side_effects=True, vmem_limit_bytes=60 * 2**20
        ),
        name="chebyshev",
    )(pair_counts.reshape(-1), meta, rhs, band, cross)
    return done[None]


def solution(mesh):
    return jax.shard_map(
        functools.partial(body, mesh.shape["line"], mesh.shape["seg"]),
        mesh=mesh,
        in_specs=(
            P("line", "seg", None, None),
            P("line", "seg", None, None, None),
            P("line", "seg", None, None, None),
            P("line", "seg", None),
            P("line", "seg", None, None, None, None),
        ),
        out_specs=P("line", "seg", None, None),
        check_vma=False,
    )
```

```python
import functools

import jax
import jax.numpy as jnp
from jax import lax
from jax.experimental import pallas as pl
from jax.experimental.pallas import tpu as pltpu
from jax.sharding import PartitionSpec as P

ITERS = 3
HALO = 3
LO_BOUND = 1.5
HI_BOUND = 12.0
MESH = pl.DeviceIdType.MESH


def kernel(lines, segs, offsets, slots, *refs):
    (count_ref, meta_vec, rhs, band_in, cross_in, out) = refs[:6]
    (wide, band, cross, ctrans, lower, meta_in, meta_far, meta_own, resid, direc, entry) = refs[6:17]
    per = [refs[17 + 6 * t : 23 + 6 * t] for t in range(ITERS)]
    send_sem, recv_sem, local_sem = refs[17 + 6 * ITERS :]
    knots, params, probes = resid.shape
    buckets = len(offsets)
    line = lax.axis_index("line")
    seg = lax.axis_index("seg")
    has_prev = seg > 0
    has_next = seg < segs - 1

    def line_at(shift):
        return (lax.rem(line + (shift + lines), lines), seg)

    prev_dev = (line, jnp.maximum(seg - 1, 0))
    next_dev = (line, jnp.minimum(seg + 1, segs - 1))

    barrier = pltpu.get_barrier_semaphore()
    for off in offsets:
        pl.semaphore_signal(barrier, inc=1, device_id=line_at(off), device_id_type=MESH)

    @pl.when(has_prev)
    def _():
        pl.semaphore_signal(barrier, inc=1, device_id=prev_dev, device_id_type=MESH)

    @pl.when(has_next)
    def _():
        pl.semaphore_signal(barrier, inc=1, device_id=next_dev, device_id_type=MESH)

    load_rhs = pltpu.make_async_copy(rhs, resid, local_sem.at[0])
    load_cross = pltpu.make_async_copy(cross_in, cross, local_sem.at[1])
    load_band = pltpu.make_async_copy(band_in, band, local_sem.at[2])
    load_own = pltpu.make_async_copy(meta_vec, meta_own, local_sem.at[3])
    load_rhs.start()
    load_own.start()
    load_cross.start()
    load_band.start()

    center = (HI_BOUND + LO_BOUND) / 2.0
    radius = (HI_BOUND - LO_BOUND) / 2.0
    coeff = radius / center

    load_rhs.wait()
    for k in range(knots):
        first = resid[k] / center
        direc[k] = first
        out[k] = first
        per[0][0][k] = first.astype(jnp.bfloat16)

    pl.semaphore_wait(
        barrier, buckets + has_prev.astype(jnp.int32) + has_next.astype(jnp.int32)
    )

    def remote(src, dst, sem, device):
        return pltpu.make_async_remote_copy(
            src_ref=src,
            dst_ref=dst,
            send_sem=send_sem.at[sem],
            recv_sem=recv_sem.at[sem],
            device_id=device,
            device_id_type=MESH,
        )

    meta_copies = [
        remote(meta_vec, meta_in.at[b], b, line_at(off)) for b, off in enumerate(offsets)
    ]
    for copy in meta_copies:
        copy.start()
    lower_copy = remote(band_in.at[pl.ds(knots - HALO, HALO)], lower, buckets, next_dev)
    base = buckets + 1
    stride = 2 * buckets + 2

    def halo_copies(t):
        own, ext = per[t][0], per[t][1]
        at = base + t * stride
        up = remote(own.at[pl.ds(knots - HALO, HALO)], ext.at[pl.ds(0, HALO)], at, next_dev)
        down = remote(own.at[pl.ds(0, HALO)], ext.at[pl.ds(HALO + knots, HALO)], at + 1, prev_dev)
        return up, down

    def start_halos(t):
        up, down = halo_copies(t)

        @pl.when(has_next)
        def _():
            up.start()

        @pl.when(has_prev)
        def _():
            down.start()

    def own_index(b, s, which):
        return jnp.clip(meta_own[s, which, b], 0, knots - 1)

    def far_index(b, s):
        return jnp.clip(meta_far[b, s, 1, b], 0, knots - 1)

    def asked_copies(t):
        at = base + t * stride + 2
        return [
            remote(per[t][2].at[b], per[t][4].at[b], at + b, line_at(-off))
            for b, off in enumerate(offsets)
        ]

    def product_copies(t):
        at = base + t * stride + 2 + buckets
        return [
            remote(per[t][3].at[b], per[t][5].at[b], at + b, line_at(off))
            for b, off in enumerate(offsets)
        ]

    def start_asked(t):
        for b, copy in enumerate(asked_copies(t)):
            for s in range(slots):
                per[t][2][b, s] = per[t][0][far_index(b, s)]
            copy.start()

    def start_products(t):
        for b, copy in enumerate(product_copies(t)):
            for s in range(slots):
                if t == 0:
                    keep = s < count_ref[b]
                    block = cross[b * slots + s]
                    block = jnp.where(keep, block, jnp.zeros_like(block))
                    cross[b * slots + s] = block
                    ctrans[b * slots + s] = block.T
                per[t][3][b, s] = jnp.dot(
                    ctrans[b * slots + s],
                    per[t][0][own_index(b, s, 0)],
                    preferred_element_type=jnp.float32,
                ).astype(jnp.bfloat16)
            copy.start()

    start_halos(0)

    @pl.when(has_next)
    def _():
        lower_copy.start()

    load_own.wait()
    load_cross.wait()
    start_products(0)
    for copy in meta_copies:
        copy.wait_recv()
    to_scalar = pltpu.make_async_copy(meta_in, meta_far, local_sem.at[4])
    to_scalar.start()
    to_scalar.wait()
    start_asked(0)

    load_band.wait()
    for k in range(knots):
        for step in range(HALO + 1):
            at = (HALO + step) * params
            wide[k, :, at : at + params] = band[k, step]
        for step in range(1, min(k, HALO) + 1):
            at = (HALO - step) * params
            wide[k, :, at : at + params] = band[k - step, step].T

    @pl.when(has_prev)
    def _():
        lower_copy.wait_recv()

    @pl.when(jnp.logical_not(has_prev))
    def _():
        lower[...] = jnp.zeros_like(lower)

    for k in range(HALO):
        for step in range(k + 1, HALO + 1):
            at = (HALO - step) * params
            wide[k, :, at : at + params] = lower[HALO + k - step, step].T

    for t in range(ITERS):
        own, ext, sent_v, sent_p, got_v, got_p = per[t]
        up, down = halo_copies(t)
        ext[pl.ds(HALO, knots)] = own[...]

        @pl.when(has_prev)
        def _():
            up.wait_recv()

        @pl.when(jnp.logical_not(has_prev))
        def _():
            ext[pl.ds(0, HALO)] = jnp.zeros((HALO, params, probes), jnp.bfloat16)

        @pl.when(has_next)
        def _():
            down.wait_recv()

        @pl.when(jnp.logical_not(has_next))
        def _():
            ext[pl.ds(HALO + knots, HALO)] = jnp.zeros((HALO, params, probes), jnp.bfloat16)

        for k in range(knots):
            near = ext[pl.ds(k, 2 * HALO + 1)].reshape((2 * HALO + 1) * params, probes)
            resid[k] = resid[k] - jnp.dot(wide[k], near, preferred_element_type=jnp.float32)

        def scatter(targets):
            for k in range(knots):
                total = resid[k]
                for e, target in enumerate(targets):
                    total = total - jnp.where(target == k, entry[e], 0.0)
                resid[k] = total

        def add_asked():
            for copy in asked_copies(t):
                copy.wait_recv()
            for b in range(buckets):
                for s in range(slots):
                    e = b * slots + s
                    entry[e] = jnp.dot(cross[e], got_v[b, s], preferred_element_type=jnp.float32)
            scatter([own_index(b, s, 0) for b in range(buckets) for s in range(slots)])

        def add_products():
            for copy in product_copies(t):
                copy.wait_recv()
            for b in range(buckets):
                for s in range(slots):
                    entry[b * slots + s] = got_p[b, s].astype(jnp.float32)
            scatter([far_index(b, s) for b in range(buckets) for s in range(slots)])

        if t == 0:
            add_products()
            add_asked()
        else:
            add_asked()
            add_products()
        coeff_next = 1.0 / (2.0 * center / radius - coeff)
        for k in range(knots):
            fresh = (coeff_next * coeff) * direc[k] + (2.0 * coeff_next / radius) * resid[k]
            out[k] = out[k] + fresh
            if t + 1 < ITERS:
                direc[k] = fresh
                per[t + 1][0][k] = fresh.astype(jnp.bfloat16)
        coeff = coeff_next
        if t + 1 < ITERS:
            start_halos(t + 1)
            start_asked(t + 1)
            start_products(t + 1)

    for copy in meta_copies:
        copy.wait_send()
    for t in range(ITERS):
        for copy in asked_copies(t) + product_copies(t):
            copy.wait_send()

    @pl.when(has_next)
    def _():
        lower_copy.wait_send()
        for t in range(ITERS):
            halo_copies(t)[0].wait_send()

    @pl.when(has_prev)
    def _():
        for t in range(ITERS):
            halo_copies(t)[1].wait_send()


def body(lines, segs, right_side, band_blocks, knot_pairs, pair_counts, cross_blocks):
    rhs = right_side[0]
    band = band_blocks[0]
    pairs = knot_pairs[0, 0]
    buckets, slots = pairs.shape[:2]
    knots, params, probes = rhs.shape
    cross = cross_blocks.reshape(buckets * slots, params, params)
    group = buckets // 2 + 1
    offsets = [b - (group - 1) if b < group - 1 else b - group + 2 for b in range(buckets)]
    meta = jnp.transpose(pairs, (1, 2, 0))
    half = jnp.bfloat16
    per = [
        pltpu.VMEM((knots, params, probes), half),
        pltpu.VMEM((knots + 2 * HALO, params, probes), half),
        pltpu.VMEM((buckets, slots, params, probes), half),
        pltpu.VMEM((buckets, slots, params, probes), half),
        pltpu.VMEM((buckets, slots, params, probes), half),
        pltpu.VMEM((buckets, slots, params, probes), half),
    ]
    sems = buckets + 1 + ITERS * (2 * buckets + 2)
    vmem = pl.BlockSpec(memory_space=pltpu.VMEM)
    hbm = pl.BlockSpec(memory_space=pltpu.HBM)
    smem = pl.BlockSpec(memory_space=pltpu.SMEM)
    done = pl.pallas_call(
        functools.partial(kernel, lines, segs, offsets, slots),
        out_shape=jax.ShapeDtypeStruct(rhs.shape, jnp.float32),
        in_specs=[smem, hbm, hbm, hbm, hbm],
        out_specs=vmem,
        scratch_shapes=[
            pltpu.VMEM((knots, params, (2 * HALO + 1) * params), half),
            pltpu.VMEM(band.shape, half),
            pltpu.VMEM(cross.shape, half),
            pltpu.VMEM(cross.shape, half),
            pltpu.VMEM((HALO, HALO + 1, params, params), half),
            pltpu.VMEM((buckets, *meta.shape), jnp.int32),
            pltpu.SMEM((buckets, *meta.shape), jnp.int32),
            pltpu.SMEM(meta.shape, jnp.int32),
            pltpu.VMEM(rhs.shape, jnp.float32),
            pltpu.VMEM(rhs.shape, jnp.float32),
            pltpu.VMEM((buckets * slots, params, probes), jnp.float32),
            *(per * ITERS),
            pltpu.SemaphoreType.DMA((sems,)),
            pltpu.SemaphoreType.DMA((sems,)),
            pltpu.SemaphoreType.DMA((5,)),
        ],
        compiler_params=pltpu.CompilerParams(
            collective_id=0, has_side_effects=True, vmem_limit_bytes=60 * 2**20
        ),
        name="chebyshev",
    )(pair_counts.reshape(-1), meta, rhs, band, cross)
    return done[None]


def solution(mesh):
    return jax.shard_map(
        functools.partial(body, mesh.shape["line"], mesh.shape["seg"]),
        mesh=mesh,
        in_specs=(
            P("line", "seg", None, None),
            P("line", "seg", None, None, None),
            P("line", "seg", None, None, None),
            P("line", "seg", None),
            P("line", "seg", None, None, None, None),
        ),
        out_specs=P("line", "seg", None, None),
        check_vma=False,
    )
```

```python
import functools

import jax
import jax.numpy as jnp
from jax import lax
from jax.experimental import pallas as pl
from jax.experimental.pallas import tpu as pltpu
from jax.sharding import PartitionSpec as P

ITERS = 3
HALO = 3
LO_BOUND = 1.5
HI_BOUND = 12.0
MESH = pl.DeviceIdType.MESH


def kernel(lines, segs, offsets, slots, *refs):
    (count_ref, meta_vec, rhs, band_in, cross_in, out) = refs[:6]
    (wide, band, cross, ctrans, lower, meta_in, meta_far, meta_own, resid, direc, entry) = refs[6:17]
    per = [refs[17 + 6 * t : 23 + 6 * t] for t in range(ITERS)]
    send_sem, recv_sem, local_sem = refs[17 + 6 * ITERS :]
    knots, params, probes = resid.shape
    buckets = len(offsets)
    line = lax.axis_index("line")
    seg = lax.axis_index("seg")
    has_prev = seg > 0
    has_next = seg < segs - 1

    def line_at(shift):
        return (lax.rem(line + (shift + lines), lines), seg)

    prev_dev = (line, jnp.maximum(seg - 1, 0))
    next_dev = (line, jnp.minimum(seg + 1, segs - 1))

    barrier = pltpu.get_barrier_semaphore()
    for off in offsets:
        pl.semaphore_signal(barrier, inc=1, device_id=line_at(off), device_id_type=MESH)

    @pl.when(has_prev)
    def _():
        pl.semaphore_signal(barrier, inc=1, device_id=prev_dev, device_id_type=MESH)

    @pl.when(has_next)
    def _():
        pl.semaphore_signal(barrier, inc=1, device_id=next_dev, device_id_type=MESH)

    load_rhs = pltpu.make_async_copy(rhs, resid, local_sem.at[0])
    load_cross = pltpu.make_async_copy(cross_in, cross, local_sem.at[1])
    load_band = pltpu.make_async_copy(band_in, band, local_sem.at[2])
    load_own = pltpu.make_async_copy(meta_vec, meta_own, local_sem.at[3])
    load_rhs.start()
    load_own.start()
    load_cross.start()
    load_band.start()

    center = (HI_BOUND + LO_BOUND) / 2.0
    radius = (HI_BOUND - LO_BOUND) / 2.0
    coeff = radius / center

    load_rhs.wait()
    for k in range(knots):
        first = resid[k] / center
        direc[k] = first
        out[k] = first
        per[0][0][k] = first.astype(jnp.bfloat16)

    pl.semaphore_wait(
        barrier, buckets + has_prev.astype(jnp.int32) + has_next.astype(jnp.int32)
    )

    def remote(src, dst, sem, device):
        return pltpu.make_async_remote_copy(
            src_ref=src,
            dst_ref=dst,
            send_sem=send_sem.at[sem],
            recv_sem=recv_sem.at[sem],
            device_id=device,
            device_id_type=MESH,
        )

    meta_copies = [
        remote(meta_vec, meta_in.at[b], b, line_at(off)) for b, off in enumerate(offsets)
    ]
    for copy in meta_copies:
        copy.start()
    lower_copy = remote(band_in.at[pl.ds(knots - HALO, HALO)], lower, buckets, next_dev)
    base = buckets + 1
    stride = 2 * buckets + 2

    def halo_copies(t):
        own, ext = per[t][0], per[t][1]
        at = base + t * stride
        up = remote(own.at[pl.ds(knots - HALO, HALO)], ext.at[pl.ds(0, HALO)], at, next_dev)
        down = remote(own.at[pl.ds(0, HALO)], ext.at[pl.ds(HALO + knots, HALO)], at + 1, prev_dev)
        return up, down

    def start_halos(t):
        up, down = halo_copies(t)

        @pl.when(has_next)
        def _():
            up.start()

        @pl.when(has_prev)
        def _():
            down.start()

    def own_index(b, s, which):
        return jnp.clip(meta_own[s, which, b], 0, knots - 1)

    def far_index(b, s):
        return jnp.clip(meta_far[b, s, 1, b], 0, knots - 1)

    def asked_copies(t):
        at = base + t * stride + 2
        return [
            remote(per[t][2].at[b], per[t][4].at[b], at + b, line_at(-off))
            for b, off in enumerate(offsets)
        ]

    def product_copies(t):
        at = base + t * stride + 2 + buckets
        return [
            remote(per[t][3].at[b], per[t][5].at[b], at + b, line_at(off))
            for b, off in enumerate(offsets)
        ]

    def start_asked(t):
        for b, copy in enumerate(asked_copies(t)):
            for s in range(slots):
                per[t][2][b, s] = per[t][0][far_index(b, s)]
            copy.start()

    def start_products(t):
        for b, copy in enumerate(product_copies(t)):
            for s in range(slots):
                if t == 0:
                    keep = s < count_ref[b]
                    block = cross[b * slots + s]
                    block = jnp.where(keep, block, jnp.zeros_like(block))
                    cross[b * slots + s] = block
                    ctrans[b * slots + s] = block.T
                per[t][3][b, s] = jnp.dot(
                    ctrans[b * slots + s],
                    per[t][0][own_index(b, s, 0)],
                    preferred_element_type=jnp.float32,
                ).astype(jnp.bfloat16)
            copy.start()

    start_halos(0)

    @pl.when(has_next)
    def _():
        lower_copy.start()

    load_own.wait()
    load_cross.wait()
    start_products(0)
    for copy in meta_copies:
        copy.wait_recv()
    to_scalar = pltpu.make_async_copy(meta_in, meta_far, local_sem.at[4])
    to_scalar.start()
    to_scalar.wait()
    start_asked(0)

    load_band.wait()
    for k in range(knots):
        for step in range(HALO + 1):
            at = (HALO + step) * params
            wide[k, :, at : at + params] = band[k, step]
        for step in range(1, min(k, HALO) + 1):
            at = (HALO - step) * params
            wide[k, :, at : at + params] = band[k - step, step].T

    @pl.when(has_prev)
    def _():
        lower_copy.wait_recv()

    @pl.when(jnp.logical_not(has_prev))
    def _():
        lower[...] = jnp.zeros_like(lower)

    for k in range(HALO):
        for step in range(k + 1, HALO + 1):
            at = (HALO - step) * params
            wide[k, :, at : at + params] = lower[HALO + k - step, step].T

    for t in range(ITERS):
        own, ext, sent_v, sent_p, got_v, got_p = per[t]
        up, down = halo_copies(t)
        ext[pl.ds(HALO, knots)] = own[...]

        @pl.when(has_prev)
        def _():
            up.wait_recv()

        @pl.when(jnp.logical_not(has_prev))
        def _():
            ext[pl.ds(0, HALO)] = jnp.zeros((HALO, params, probes), jnp.bfloat16)

        @pl.when(has_next)
        def _():
            down.wait_recv()

        @pl.when(jnp.logical_not(has_next))
        def _():
            ext[pl.ds(HALO + knots, HALO)] = jnp.zeros((HALO, params, probes), jnp.bfloat16)

        for k in range(knots):
            near = ext[pl.ds(k, 2 * HALO + 1)].reshape((2 * HALO + 1) * params, probes)
            resid[k] = resid[k] - jnp.dot(wide[k], near, preferred_element_type=jnp.float32)

        coeff_next = 1.0 / (2.0 * center / radius - coeff)

        def scatter(targets, last):
            for k in range(knots):
                total = resid[k]
                for e, target in enumerate(targets):
                    total = total - jnp.where(target == k, entry[e], 0.0)
                if not last or t + 1 < ITERS:
                    resid[k] = total
                if last:
                    fresh = (coeff_next * coeff) * direc[k] + (2.0 * coeff_next / radius) * total
                    out[k] = out[k] + fresh
                    if t + 1 < ITERS:
                        direc[k] = fresh
                        per[t + 1][0][k] = fresh.astype(jnp.bfloat16)

        def add_asked(last):
            for copy in asked_copies(t):
                copy.wait_recv()
            for b in range(buckets):
                for s in range(slots):
                    e = b * slots + s
                    entry[e] = jnp.dot(cross[e], got_v[b, s], preferred_element_type=jnp.float32)
            scatter([own_index(b, s, 0) for b in range(buckets) for s in range(slots)], last)

        def add_products(last):
            for copy in product_copies(t):
                copy.wait_recv()
            for b in range(buckets):
                for s in range(slots):
                    entry[b * slots + s] = got_p[b, s].astype(jnp.float32)
            scatter([far_index(b, s) for b in range(buckets) for s in range(slots)], last)

        if t == 0:
            add_products(False)
            add_asked(True)
        else:
            add_asked(False)
            add_products(True)
        coeff = coeff_next
        if t + 1 < ITERS:
            start_halos(t + 1)
            start_asked(t + 1)
            start_products(t + 1)

    for copy in meta_copies:
        copy.wait_send()
    for t in range(ITERS):
        for copy in asked_copies(t) + product_copies(t):
            copy.wait_send()

    @pl.when(has_next)
    def _():
        lower_copy.wait_send()
        for t in range(ITERS):
            halo_copies(t)[0].wait_send()

    @pl.when(has_prev)
    def _():
        for t in range(ITERS):
            halo_copies(t)[1].wait_send()


def body(lines, segs, right_side, band_blocks, knot_pairs, pair_counts, cross_blocks):
    rhs = right_side[0]
    band = band_blocks[0]
    pairs = knot_pairs[0, 0]
    buckets, slots = pairs.shape[:2]
    knots, params, probes = rhs.shape
    cross = cross_blocks.reshape(buckets * slots, params, params)
    group = buckets // 2 + 1
    offsets = [b - (group - 1) if b < group - 1 else b - group + 2 for b in range(buckets)]
    meta = jnp.transpose(pairs, (1, 2, 0))
    half = jnp.bfloat16
    per = [
        pltpu.VMEM((knots, params, probes), half),
        pltpu.VMEM((knots + 2 * HALO, params, probes), half),
        pltpu.VMEM((buckets, slots, params, probes), half),
        pltpu.VMEM((buckets, slots, params, probes), half),
        pltpu.VMEM((buckets, slots, params, probes), half),
        pltpu.VMEM((buckets, slots, params, probes), half),
    ]
    sems = buckets + 1 + ITERS * (2 * buckets + 2)
    vmem = pl.BlockSpec(memory_space=pltpu.VMEM)
    hbm = pl.BlockSpec(memory_space=pltpu.HBM)
    smem = pl.BlockSpec(memory_space=pltpu.SMEM)
    done = pl.pallas_call(
        functools.partial(kernel, lines, segs, offsets, slots),
        out_shape=pltpu.VMEM(rhs.shape, jnp.float32),
        in_specs=[smem, hbm, hbm, hbm, hbm],
        out_specs=vmem,
        scratch_shapes=[
            pltpu.VMEM((knots, params, (2 * HALO + 1) * params), half),
            pltpu.VMEM(band.shape, half),
            pltpu.VMEM(cross.shape, half),
            pltpu.VMEM(cross.shape, half),
            pltpu.VMEM((HALO, HALO + 1, params, params), half),
            pltpu.VMEM((buckets, *meta.shape), jnp.int32),
            pltpu.SMEM((buckets, *meta.shape), jnp.int32),
            pltpu.SMEM(meta.shape, jnp.int32),
            pltpu.VMEM(rhs.shape, jnp.float32),
            pltpu.VMEM(rhs.shape, jnp.float32),
            pltpu.VMEM((buckets * slots, params, probes), jnp.float32),
            *(per * ITERS),
            pltpu.SemaphoreType.DMA((sems,)),
            pltpu.SemaphoreType.DMA((sems,)),
            pltpu.SemaphoreType.DMA((5,)),
        ],
        compiler_params=pltpu.CompilerParams(
            collective_id=0, has_side_effects=True, vmem_limit_bytes=56 * 2**20
        ),
        name="chebyshev",
    )(pair_counts.reshape(-1), meta, rhs, band, cross)
    return done[None]


def solution(mesh):
    return jax.shard_map(
        functools.partial(body, mesh.shape["line"], mesh.shape["seg"]),
        mesh=mesh,
        in_specs=(
            P("line", "seg", None, None),
            P("line", "seg", None, None, None),
            P("line", "seg", None, None, None),
            P("line", "seg", None),
            P("line", "seg", None, None, None, None),
        ),
        out_specs=P("line", "seg", None, None),
        check_vma=False,
    )
```

```python
import functools

import jax
import jax.numpy as jnp
from jax import lax
from jax.experimental import pallas as pl
from jax.experimental.pallas import tpu as pltpu
from jax.sharding import PartitionSpec as P

ITERS = 3
HALO = 3
LO_BOUND = 1.5
HI_BOUND = 12.0
MESH = pl.DeviceIdType.MESH


def kernel(lines, segs, offsets, slots, *refs):
    (count_ref, meta_vec, rhs, band_in, cross_in, out) = refs[:6]
    (wide, band, cross, ctrans, lower, meta_in, meta_far, meta_own, resid, direc, entry) = refs[6:17]
    per = [refs[17 + 7 * t : 24 + 7 * t] for t in range(ITERS)]
    send_sem, recv_sem, local_sem = refs[17 + 7 * ITERS :]
    knots, params, probes = resid.shape
    buckets = len(offsets)
    line = lax.axis_index("line")
    seg = lax.axis_index("seg")
    has_prev = seg > 0
    has_next = seg < segs - 1

    def line_at(shift):
        return (lax.rem(line + (shift + lines), lines), seg)

    prev_dev = (line, jnp.maximum(seg - 1, 0))
    next_dev = (line, jnp.minimum(seg + 1, segs - 1))

    barrier = pltpu.get_barrier_semaphore()
    for off in offsets:
        pl.semaphore_signal(barrier, inc=1, device_id=line_at(off), device_id_type=MESH)

    @pl.when(has_prev)
    def _():
        pl.semaphore_signal(barrier, inc=1, device_id=prev_dev, device_id_type=MESH)

    @pl.when(has_next)
    def _():
        pl.semaphore_signal(barrier, inc=1, device_id=next_dev, device_id_type=MESH)

    load_rhs = pltpu.make_async_copy(rhs, resid, local_sem.at[0])
    load_cross = pltpu.make_async_copy(cross_in, cross, local_sem.at[1])
    load_band = pltpu.make_async_copy(band_in, band, local_sem.at[2])
    load_own = pltpu.make_async_copy(meta_vec, meta_own, local_sem.at[3])
    load_rhs.start()
    load_own.start()
    load_cross.start()
    load_band.start()

    center = (HI_BOUND + LO_BOUND) / 2.0
    radius = (HI_BOUND - LO_BOUND) / 2.0
    coeff = radius / center

    load_rhs.wait()
    for k in range(knots):
        first = resid[k] / center
        direc[k] = first
        out[k] = first
        per[0][6][k] = first.astype(jnp.bfloat16)

    pl.semaphore_wait(
        barrier, buckets + has_prev.astype(jnp.int32) + has_next.astype(jnp.int32)
    )

    def remote(src, dst, sem, device):
        return pltpu.make_async_remote_copy(
            src_ref=src,
            dst_ref=dst,
            send_sem=send_sem.at[sem],
            recv_sem=recv_sem.at[sem],
            device_id=device,
            device_id_type=MESH,
        )

    meta_copies = [
        remote(meta_vec, meta_in.at[b], b, line_at(off)) for b, off in enumerate(offsets)
    ]
    for copy in meta_copies:
        copy.start()
    lower_copy = remote(band_in.at[pl.ds(knots - HALO, HALO)], lower, buckets, next_dev)
    base = buckets + 1
    stride = 4 * buckets + 2
    lane = lax.broadcasted_iota(jnp.int32, (params, probes), 1)
    split = probes // 2
    sides = [lane < split, lane >= split]

    def halo_copies(t):
        own, ext = per[t][6], per[t][1]
        at = base + t * stride
        up = remote(own.at[pl.ds(knots - HALO, HALO)], ext.at[pl.ds(0, HALO)], at, next_dev)
        down = remote(own.at[pl.ds(0, HALO)], ext.at[pl.ds(HALO + knots, HALO)], at + 1, prev_dev)
        return up, down

    def start_halos(t):
        up, down = halo_copies(t)

        @pl.when(has_next)
        def _():
            up.start()

        @pl.when(has_prev)
        def _():
            down.start()

    def own_index(b, s, which):
        return jnp.clip(meta_own[s, which, b], 0, knots - 1)

    def far_index(b, s):
        return jnp.clip(meta_far[b, s, 1, b], 0, knots - 1)

    def asked_copies(t, h):
        at = base + t * stride + 2 + 2 * h * buckets
        return [
            remote(per[t][2].at[h, b], per[t][4].at[h, b], at + b, line_at(-off))
            for b, off in enumerate(offsets)
        ]

    def product_copies(t, h):
        at = base + t * stride + 2 + (2 * h + 1) * buckets
        return [
            remote(per[t][3].at[h, b], per[t][5].at[h, b], at + b, line_at(off))
            for b, off in enumerate(offsets)
        ]

    def source(t, h):
        return per[t][0 if h == 0 and t > 0 else 6]

    def packed(h, blocks):
        first, second = blocks
        if h == 0:
            second = pltpu.roll(second, split, 1)
        else:
            first = pltpu.roll(first, split, 1)
        return jnp.where(sides[0], first, second).astype(jnp.bfloat16)

    def unpacked(h, s, block):
        if s != h:
            block = pltpu.roll(block, split, 1)
        return jnp.where(sides[h], block, 0.0)

    def start_asked(t, h):
        for b, copy in enumerate(asked_copies(t, h)):
            blocks = [source(t, h)[far_index(b, s)].astype(jnp.float32) for s in range(slots)]
            per[t][2][h, b] = packed(h, blocks)
            copy.start()

    def start_products(t, h):
        for b, copy in enumerate(product_copies(t, h)):
            blocks = []
            for s in range(slots):
                if t == 0 and h == 0:
                    keep = s < count_ref[b]
                    block = cross[b * slots + s]
                    block = jnp.where(keep, block, jnp.zeros_like(block))
                    cross[b * slots + s] = block
                    ctrans[b * slots + s] = block.T
                blocks.append(
                    jnp.dot(
                        ctrans[b * slots + s],
                        source(t, h)[own_index(b, s, 0)],
                        preferred_element_type=jnp.float32,
                    )
                )
            per[t][3][h, b] = packed(h, blocks)
            copy.start()

    start_halos(0)

    @pl.when(has_next)
    def _():
        lower_copy.start()

    load_own.wait()
    load_cross.wait()
    start_products(0, 0)
    for copy in meta_copies:
        copy.wait_recv()
    to_scalar = pltpu.make_async_copy(meta_in, meta_far, local_sem.at[4])
    to_scalar.start()
    to_scalar.wait()
    start_asked(0, 0)
    start_products(0, 1)
    start_asked(0, 1)

    load_band.wait()
    for k in range(knots):
        for step in range(HALO + 1):
            at = (HALO + step) * params
            wide[k, :, at : at + params] = band[k, step]
        for step in range(1, min(k, HALO) + 1):
            at = (HALO - step) * params
            wide[k, :, at : at + params] = band[k - step, step].T

    @pl.when(has_prev)
    def _():
        lower_copy.wait_recv()

    @pl.when(jnp.logical_not(has_prev))
    def _():
        lower[...] = jnp.zeros_like(lower)

    for k in range(HALO):
        for step in range(k + 1, HALO + 1):
            at = (HALO - step) * params
            wide[k, :, at : at + params] = lower[HALO + k - step, step].T

    for t in range(ITERS):
        _, ext, _, _, got_v, got_p, own = per[t]
        up, down = halo_copies(t)
        ext[pl.ds(HALO, knots)] = own[...]

        @pl.when(has_prev)
        def _():
            up.wait_recv()

        @pl.when(jnp.logical_not(has_prev))
        def _():
            ext[pl.ds(0, HALO)] = jnp.zeros((HALO, params, probes), jnp.bfloat16)

        @pl.when(has_next)
        def _():
            down.wait_recv()

        @pl.when(jnp.logical_not(has_next))
        def _():
            ext[pl.ds(HALO + knots, HALO)] = jnp.zeros((HALO, params, probes), jnp.bfloat16)

        for k in range(knots):
            near = ext[pl.ds(k, 2 * HALO + 1)].reshape((2 * HALO + 1) * params, probes)
            resid[k] = resid[k] - jnp.dot(wide[k], near, preferred_element_type=jnp.float32)

        coeff_next = 1.0 / (2.0 * center / radius - coeff)

        coeff_next = 1.0 / (2.0 * center / radius - coeff)

        def scatter(targets):
            for k in range(knots):
                total = resid[k]
                for e, target in enumerate(targets):
                    total = total - jnp.where(target == k, entry[e], 0.0)
                resid[k] = total

        def add_asked(h):
            for copy in asked_copies(t, h):
                copy.wait_recv()
            for b in range(buckets):
                for s in range(slots):
                    e = b * slots + s
                    term = jnp.dot(cross[e], got_v[h, b], preferred_element_type=jnp.float32)
                    entry[e] = unpacked(h, s, term)
            scatter([own_index(b, s, 0) for b in range(buckets) for s in range(slots)])

        def add_products(h):
            for copy in product_copies(t, h):
                copy.wait_recv()
            for b in range(buckets):
                for s in range(slots):
                    entry[b * slots + s] = unpacked(h, s, got_p[h, b].astype(jnp.float32))
            scatter([far_index(b, s) for b in range(buckets) for s in range(slots)])

        for h in range(2):
            if t == 0:
                add_products(h)
                add_asked(h)
            else:
                add_asked(h)
                add_products(h)
            for k in range(knots):
                old = direc[k]
                fresh = (coeff_next * coeff) * old + (2.0 * coeff_next / radius) * resid[k]
                out[k] = out[k] + jnp.where(sides[h], fresh, 0.0)
                if t + 1 < ITERS:
                    fresh = jnp.where(sides[h], fresh, old)
                    direc[k] = fresh
                    per[t + 1][0 if h == 0 else 6][k] = fresh.astype(jnp.bfloat16)
            if t + 1 < ITERS:
                if h == 1:
                    start_halos(t + 1)
                start_asked(t + 1, h)
                start_products(t + 1, h)
        coeff = coeff_next

    for copy in meta_copies:
        copy.wait_send()
    for t in range(ITERS):
        for h in range(2):
            for copy in asked_copies(t, h) + product_copies(t, h):
                copy.wait_send()

    @pl.when(has_next)
    def _():
        lower_copy.wait_send()
        for t in range(ITERS):
            halo_copies(t)[0].wait_send()

    @pl.when(has_prev)
    def _():
        for t in range(ITERS):
            halo_copies(t)[1].wait_send()


def body(lines, segs, right_side, band_blocks, knot_pairs, pair_counts, cross_blocks):
    rhs = right_side[0]
    band = band_blocks[0]
    pairs = knot_pairs[0, 0]
    buckets, slots = pairs.shape[:2]
    knots, params, probes = rhs.shape
    cross = cross_blocks.reshape(buckets * slots, params, params)
    group = buckets // 2 + 1
    offsets = [b - (group - 1) if b < group - 1 else b - group + 2 for b in range(buckets)]
    meta = jnp.transpose(pairs, (1, 2, 0))
    half = jnp.bfloat16
    per = [
        pltpu.VMEM((knots, params, probes), half),
        pltpu.VMEM((knots + 2 * HALO, params, probes), half),
        *([pltpu.VMEM((2, buckets, params, probes), half)] * 4),
        pltpu.VMEM((knots, params, probes), half),
    ]
    sems = buckets + 1 + ITERS * (4 * buckets + 2)
    vmem = pl.BlockSpec(memory_space=pltpu.VMEM)
    hbm = pl.BlockSpec(memory_space=pltpu.HBM)
    smem = pl.BlockSpec(memory_space=pltpu.SMEM)
    done = pl.pallas_call(
        functools.partial(kernel, lines, segs, offsets, slots),
        out_shape=pltpu.VMEM(rhs.shape, jnp.float32),
        in_specs=[smem, hbm, hbm, hbm, hbm],
        out_specs=vmem,
        scratch_shapes=[
            pltpu.VMEM((knots, params, (2 * HALO + 1) * params), half),
            pltpu.VMEM(band.shape, half),
            pltpu.VMEM(cross.shape, half),
            pltpu.VMEM(cross.shape, half),
            pltpu.VMEM((HALO, HALO + 1, params, params), half),
            pltpu.VMEM((buckets, *meta.shape), jnp.int32),
            pltpu.SMEM((buckets, *meta.shape), jnp.int32),
            pltpu.SMEM(meta.shape, jnp.int32),
            pltpu.VMEM(rhs.shape, jnp.float32),
            pltpu.VMEM(rhs.shape, jnp.float32),
            pltpu.VMEM((buckets * slots, params, probes), jnp.float32),
            *(per * ITERS),
            pltpu.SemaphoreType.DMA((sems,)),
            pltpu.SemaphoreType.DMA((sems,)),
            pltpu.SemaphoreType.DMA((5,)),
        ],
        compiler_params=pltpu.CompilerParams(
            collective_id=0, has_side_effects=True, vmem_limit_bytes=56 * 2**20
        ),
        name="chebyshev",
    )(pair_counts.reshape(-1), meta, rhs, band, cross)
    return done[None]


def solution(mesh):
    return jax.shard_map(
        functools.partial(body, mesh.shape["line"], mesh.shape["seg"]),
        mesh=mesh,
        in_specs=(
            P("line", "seg", None, None),
            P("line", "seg", None, None, None),
            P("line", "seg", None, None, None),
            P("line", "seg", None),
            P("line", "seg", None, None, None, None),
        ),
        out_specs=P("line", "seg", None, None),
        check_vma=False,
    )
```

```python
import functools

import jax
import jax.numpy as jnp
from jax import lax
from jax.experimental import pallas as pl
from jax.experimental.pallas import tpu as pltpu
from jax.sharding import PartitionSpec as P

ITERS = 3
HALO = 3
LO_BOUND = 1.5
HI_BOUND = 12.0
MESH = pl.DeviceIdType.MESH


def kernel(lines, segs, offsets, slots, *refs):
    (count_ref, meta_vec, rhs, band_in, cross_in, out) = refs[:6]
    (wide, band, cross, ctrans, lower, meta_in, meta_far, meta_own, resid, direc, entry) = refs[6:17]
    per = [refs[17 + 7 * t : 24 + 7 * t] for t in range(ITERS)]
    send_sem, recv_sem, local_sem = refs[17 + 7 * ITERS :]
    knots, params, probes = resid.shape
    buckets = len(offsets)
    order = sorted(range(buckets), key=lambda b: (abs(offsets[b]) == 1, abs(offsets[b]), b))
    line = lax.axis_index("line")
    seg = lax.axis_index("seg")
    has_prev = seg > 0
    has_next = seg < segs - 1

    def line_at(shift):
        return (lax.rem(line + (shift + lines), lines), seg)

    prev_dev = (line, jnp.maximum(seg - 1, 0))
    next_dev = (line, jnp.minimum(seg + 1, segs - 1))

    barrier = pltpu.get_barrier_semaphore()
    for off in offsets:
        pl.semaphore_signal(barrier, inc=1, device_id=line_at(off), device_id_type=MESH)

    @pl.when(has_prev)
    def _():
        pl.semaphore_signal(barrier, inc=1, device_id=prev_dev, device_id_type=MESH)

    @pl.when(has_next)
    def _():
        pl.semaphore_signal(barrier, inc=1, device_id=next_dev, device_id_type=MESH)

    load_rhs = pltpu.make_async_copy(rhs, resid, local_sem.at[0])
    load_cross = pltpu.make_async_copy(cross_in, cross, local_sem.at[1])
    load_band = pltpu.make_async_copy(band_in, band, local_sem.at[2])
    load_own = pltpu.make_async_copy(meta_vec, meta_own, local_sem.at[3])
    load_rhs.start()
    load_own.start()
    load_cross.start()
    load_band.start()

    center = (HI_BOUND + LO_BOUND) / 2.0
    radius = (HI_BOUND - LO_BOUND) / 2.0
    coeff = radius / center

    load_rhs.wait()
    for k in range(knots):
        first = resid[k] / center
        direc[k] = first
        out[k] = first
        per[0][6][k] = first.astype(jnp.bfloat16)

    pl.semaphore_wait(
        barrier, buckets + has_prev.astype(jnp.int32) + has_next.astype(jnp.int32)
    )

    def remote(src, dst, sem, device):
        return pltpu.make_async_remote_copy(
            src_ref=src,
            dst_ref=dst,
            send_sem=send_sem.at[sem],
            recv_sem=recv_sem.at[sem],
            device_id=device,
            device_id_type=MESH,
        )

    meta_copies = [
        remote(meta_vec, meta_in.at[b], b, line_at(off)) for b, off in enumerate(offsets)
    ]
    for copy in meta_copies:
        copy.start()
    lower_copies = [
        remote(
            band_in.at[knots - HALO + j, pl.ds(HALO - j, j + 1)],
            lower.at[j, pl.ds(HALO - j, j + 1)],
            buckets + j,
            next_dev,
        )
        for j in range(HALO)
    ]
    base = buckets + HALO
    stride = 4 * buckets + 2
    lane = lax.broadcasted_iota(jnp.int32, (params, probes), 1)
    split = probes // 2
    sides = [lane < split, lane >= split]

    def halo_copies(t):
        own, ext = per[t][6], per[t][1]
        at = base + t * stride
        up = remote(own.at[pl.ds(knots - HALO, HALO)], ext.at[pl.ds(0, HALO)], at, next_dev)
        down = remote(own.at[pl.ds(0, HALO)], ext.at[pl.ds(HALO + knots, HALO)], at + 1, prev_dev)
        return up, down

    def start_halos(t):
        up, down = halo_copies(t)

        @pl.when(has_next)
        def _():
            up.start()

        @pl.when(has_prev)
        def _():
            down.start()

    def own_index(b, s, which):
        return jnp.clip(meta_own[s, which, b], 0, knots - 1)

    def far_index(b, s):
        return jnp.clip(meta_far[b, s, 1, b], 0, knots - 1)

    def asked_copies(t, h):
        at = base + t * stride + 2 + 2 * h * buckets
        return [
            remote(per[t][2].at[h, b], per[t][4].at[h, b], at + b, line_at(-off))
            for b, off in enumerate(offsets)
        ]

    def product_copies(t, h):
        at = base + t * stride + 2 + (2 * h + 1) * buckets
        return [
            remote(per[t][3].at[h, b], per[t][5].at[h, b], at + b, line_at(off))
            for b, off in enumerate(offsets)
        ]

    def source(t, h):
        return per[t][0 if h == 0 and t > 0 else 6]

    def packed(h, blocks):
        first, second = blocks
        if h == 0:
            second = pltpu.roll(second, split, 1)
        else:
            first = pltpu.roll(first, split, 1)
        return jnp.where(sides[0], first, second).astype(jnp.bfloat16)

    def unpacked(h, s, block):
        if s != h:
            block = pltpu.roll(block, split, 1)
        return jnp.where(sides[h], block, 0.0)

    def start_asked(t, h):
        copies = asked_copies(t, h)
        for b in order:
            copy = copies[b]
            blocks = [source(t, h)[far_index(b, s)].astype(jnp.float32) for s in range(slots)]
            per[t][2][h, b] = packed(h, blocks)
            copy.start()

    def start_products(t, h):
        copies = product_copies(t, h)
        for b in order:
            copy = copies[b]
            blocks = []
            for s in range(slots):
                if t == 0 and h == 0:
                    keep = s < count_ref[b]
                    block = cross[b * slots + s]
                    block = jnp.where(keep, block, jnp.zeros_like(block))
                    cross[b * slots + s] = block
                    ctrans[b * slots + s] = block.T
                blocks.append(
                    jnp.dot(
                        ctrans[b * slots + s],
                        source(t, h)[own_index(b, s, 0)],
                        preferred_element_type=jnp.float32,
                    )
                )
            per[t][3][h, b] = packed(h, blocks)
            copy.start()

    start_halos(0)

    @pl.when(has_next)
    def _():
        for copy in lower_copies:
            copy.start()

    load_own.wait()
    load_cross.wait()
    start_products(0, 0)
    for copy in meta_copies:
        copy.wait_recv()
    to_scalar = pltpu.make_async_copy(meta_in, meta_far, local_sem.at[4])
    to_scalar.start()
    to_scalar.wait()
    start_asked(0, 0)
    start_products(0, 1)
    start_asked(0, 1)

    load_band.wait()
    for k in range(knots):
        for step in range(HALO + 1):
            at = (HALO + step) * params
            wide[k, :, at : at + params] = band[k, step]
        for step in range(1, min(k, HALO) + 1):
            at = (HALO - step) * params
            wide[k, :, at : at + params] = band[k - step, step].T

    @pl.when(has_prev)
    def _():
        for copy in lower_copies:
            copy.wait_recv()

    @pl.when(jnp.logical_not(has_prev))
    def _():
        lower[...] = jnp.zeros_like(lower)

    for k in range(HALO):
        for step in range(k + 1, HALO + 1):
            at = (HALO - step) * params
            wide[k, :, at : at + params] = lower[HALO + k - step, step].T

    for t in range(ITERS):
        _, ext, _, _, got_v, got_p, own = per[t]
        up, down = halo_copies(t)
        ext[pl.ds(HALO, knots)] = own[...]

        @pl.when(has_prev)
        def _():
            up.wait_recv()

        @pl.when(jnp.logical_not(has_prev))
        def _():
            ext[pl.ds(0, HALO)] = jnp.zeros((HALO, params, probes), jnp.bfloat16)

        @pl.when(has_next)
        def _():
            down.wait_recv()

        @pl.when(jnp.logical_not(has_next))
        def _():
            ext[pl.ds(HALO + knots, HALO)] = jnp.zeros((HALO, params, probes), jnp.bfloat16)

        for k in range(knots):
            near = ext[pl.ds(k, 2 * HALO + 1)].reshape((2 * HALO + 1) * params, probes)
            resid[k] = resid[k] - jnp.dot(wide[k], near, preferred_element_type=jnp.float32)

        coeff_next = 1.0 / (2.0 * center / radius - coeff)

        coeff_next = 1.0 / (2.0 * center / radius - coeff)

        def scatter(targets):
            for k in range(knots):
                total = resid[k]
                for e, target in enumerate(targets):
                    total = total - jnp.where(target == k, entry[e], 0.0)
                resid[k] = total

        def add_asked(h):
            for copy in asked_copies(t, h):
                copy.wait_recv()
            for b in range(buckets):
                for s in range(slots):
                    e = b * slots + s
                    term = jnp.dot(cross[e], got_v[h, b], preferred_element_type=jnp.float32)
                    entry[e] = unpacked(h, s, term)
            scatter([own_index(b, s, 0) for b in range(buckets) for s in range(slots)])

        def add_products(h):
            for copy in product_copies(t, h):
                copy.wait_recv()
            for b in range(buckets):
                for s in range(slots):
                    entry[b * slots + s] = unpacked(h, s, got_p[h, b].astype(jnp.float32))
            scatter([far_index(b, s) for b in range(buckets) for s in range(slots)])

        for h in range(2):
            if t == 0:
                add_products(h)
                add_asked(h)
            else:
                add_asked(h)
                add_products(h)
            for k in range(knots):
                old = direc[k]
                fresh = (coeff_next * coeff) * old + (2.0 * coeff_next / radius) * resid[k]
                out[k] = out[k] + jnp.where(sides[h], fresh, 0.0)
                if t + 1 < ITERS:
                    fresh = jnp.where(sides[h], fresh, old)
                    direc[k] = fresh
                    per[t + 1][0 if h == 0 else 6][k] = fresh.astype(jnp.bfloat16)
            if t + 1 < ITERS:
                if h == 1:
                    start_halos(t + 1)
                start_asked(t + 1, h)
                start_products(t + 1, h)
        coeff = coeff_next

    for copy in meta_copies:
        copy.wait_send()
    for t in range(ITERS):
        for h in range(2):
            for copy in asked_copies(t, h) + product_copies(t, h):
                copy.wait_send()

    @pl.when(has_next)
    def _():
        for copy in lower_copies:
            copy.wait_send()
        for t in range(ITERS):
            halo_copies(t)[0].wait_send()

    @pl.when(has_prev)
    def _():
        for t in range(ITERS):
            halo_copies(t)[1].wait_send()


def body(lines, segs, right_side, band_blocks, knot_pairs, pair_counts, cross_blocks):
    rhs = right_side[0]
    band = band_blocks[0]
    pairs = knot_pairs[0, 0]
    buckets, slots = pairs.shape[:2]
    knots, params, probes = rhs.shape
    cross = cross_blocks.reshape(buckets * slots, params, params)
    group = buckets // 2 + 1
    offsets = [b - (group - 1) if b < group - 1 else b - group + 2 for b in range(buckets)]
    meta = jnp.transpose(pairs, (1, 2, 0))
    half = jnp.bfloat16
    per = [
        pltpu.VMEM((knots, params, probes), half),
        pltpu.VMEM((knots + 2 * HALO, params, probes), half),
        *([pltpu.VMEM((2, buckets, params, probes), half)] * 4),
        pltpu.VMEM((knots, params, probes), half),
    ]
    sems = buckets + HALO + ITERS * (4 * buckets + 2)
    vmem = pl.BlockSpec(memory_space=pltpu.VMEM)
    hbm = pl.BlockSpec(memory_space=pltpu.HBM)
    smem = pl.BlockSpec(memory_space=pltpu.SMEM)
    done = pl.pallas_call(
        functools.partial(kernel, lines, segs, offsets, slots),
        out_shape=pltpu.VMEM(rhs.shape, jnp.float32),
        in_specs=[smem, hbm, hbm, hbm, hbm],
        out_specs=vmem,
        scratch_shapes=[
            pltpu.VMEM((knots, params, (2 * HALO + 1) * params), half),
            pltpu.VMEM(band.shape, half),
            pltpu.VMEM(cross.shape, half),
            pltpu.VMEM(cross.shape, half),
            pltpu.VMEM((HALO, HALO + 1, params, params), half),
            pltpu.VMEM((buckets, *meta.shape), jnp.int32),
            pltpu.SMEM((buckets, *meta.shape), jnp.int32),
            pltpu.SMEM(meta.shape, jnp.int32),
            pltpu.VMEM(rhs.shape, jnp.float32),
            pltpu.VMEM(rhs.shape, jnp.float32),
            pltpu.VMEM((buckets * slots, params, probes), jnp.float32),
            *(per * ITERS),
            pltpu.SemaphoreType.DMA((sems,)),
            pltpu.SemaphoreType.DMA((sems,)),
            pltpu.SemaphoreType.DMA((5,)),
        ],
        compiler_params=pltpu.CompilerParams(
            collective_id=0, has_side_effects=True, vmem_limit_bytes=56 * 2**20
        ),
        name="chebyshev",
    )(pair_counts.reshape(-1), meta, rhs, band, cross)
    return done[None]


def solution(mesh):
    return jax.shard_map(
        functools.partial(body, mesh.shape["line"], mesh.shape["seg"]),
        mesh=mesh,
        in_specs=(
            P("line", "seg", None, None),
            P("line", "seg", None, None, None),
            P("line", "seg", None, None, None),
            P("line", "seg", None),
            P("line", "seg", None, None, None, None),
        ),
        out_specs=P("line", "seg", None, None),
        check_vma=False,
    )
```
